32 devices in a mesh: groups: 2 (over x), rows: 16 (over z, y, core).
Axes of the slice: x: 2, y: 2, z: 4, core: 2. Of those that a mesh axis runs over, the one named last changes fastest.
Arguments:
- latents: bfloat16 [2, 64, 256, 128], P('groups', 'rows'), parts along dimension 0, may hold values from -60 to 60
- gain_one: float32 [128], replicated, may hold values from 0.25 to 1.75
- shift_one: float32 [128], replicated, may hold values from -3 to 3
- weight_one: bfloat16 [3, 3, 3, 128, 128], replicated, may hold values from -0.109375 to 0.109375
- bias_one: float32 [128], replicated, may hold values from -3 to 3
- gain_two: float32 [128], replicated, may hold values from 0.25 to 1.75
- shift_two: float32 [128], replicated, may hold values from -3 to 3
- weight_two: bfloat16 [3, 3, 3, 128, 128], replicated, may hold values from -0.109375 to 0.109375
- bias_two: float32 [128], replicated, may hold values from -3 to 3
Outputs:
- decoded: bfloat16 [2, 64, 256, 128], P('groups', 'rows'), parts along dimension 0
The draws below stay inside these ranges and needn't reach their ends.
There are 2 independent parts, one for each index of `groups`. The reference program is written for one: setup_inputs(seed, part) draws one part's arguments, and reference() takes and returns one part's arrays. A program takes and returns all parts, laid end to end along the dimension named above; an argument that names none is the same for every part. Nothing has to cross between parts.
All inputs are finite; a program needn't handle non-finite values.
Results may differ from the reference program's by a relative error of at most 0.004.
Values may be sent and summed in bfloat16 or wider, within the bound.
A program may use at most 64 MiB of HBM per device.

```python
import jax
import jax.numpy as jnp
from jax import lax

C = 128
GROUPS = 32
FRAMES = 1
ROWS_DEV = 4
W = 256
H = 64


def draw_latents(key, part):
    key_base = jax.random.fold_in(key, 11)
    key_chan = jax.random.fold_in(key, 12)
    key_band = jax.random.fold_in(key, 14)
    key_bandshift = jax.random.fold_in(key, 15)
    shape = (FRAMES, H, W, C)
    band_count = H // ROWS_DEV
    positions = jnp.arange(H, dtype=jnp.float32) / max(H - 1, 1)
    band_level = jnp.exp(jax.random.uniform(key_band, (band_count,), jnp.float32, jnp.log(0.25), jnp.log(2.5)))
    band_offset = jax.random.normal(key_bandshift, (band_count, C), jnp.float32)
    row_level = jnp.repeat(band_level, ROWS_DEV)
    row_offset = jnp.repeat(band_offset, ROWS_DEV, axis=0)
    base = jnp.clip(jax.random.normal(key_base, shape, jnp.float32), -6.0, 6.0)
    row_scale = jnp.exp(jnp.log(3.0) * positions)
    chan_scale = jnp.exp(jax.random.uniform(key_chan, (C,), jnp.float32, jnp.log(0.3), jnp.log(3.0)))
    shifted = base + row_offset[None, :, None, :]
    values = shifted * chan_scale * (row_scale * row_level)[None, :, None, None]
    return jnp.clip(values, -60.0, 60.0).astype(jnp.bfloat16)


def scatter_about(own_key, shape, spread, reach, kind=jnp.bfloat16):
    array = spread * jax.random.normal(own_key, shape, jnp.float32)
    return jnp.clip(array, min=-reach, max=reach).astype(kind)


def setup_inputs(seed: int = 0, part: int = 0) -> dict:
    keys = jax.random.split(jax.random.key(seed), 10)
    part_keys = jax.random.split(jax.random.fold_in(keys[9], part), 10)
    return {
        "latents": draw_latents(jax.random.fold_in(jax.random.fold_in(keys[9], part), 71), part),
        "gain_one": jnp.clip(1.0 + 0.15 * jax.random.normal(keys[1], (C,), jnp.float32), 0.25, 1.75),
        "shift_one": scatter_about(keys[2], (C,), 0.5, 3.0, jnp.float32),
        "weight_one": scatter_about(keys[3], (3, 3, 3, C, C), (27 * C) ** -0.5, 0.109375),
        "bias_one": scatter_about(keys[4], (C,), 0.5, 3.0, jnp.float32),
        "gain_two": jnp.clip(1.0 + 0.15 * jax.random.normal(keys[5], (C,), jnp.float32), 0.25, 1.75),
        "shift_two": scatter_about(keys[6], (C,), 0.5, 3.0, jnp.float32),
        "weight_two": scatter_about(keys[7], (3, 3, 3, C, C), (27 * C) ** -0.5, 0.109375),
        "bias_two": scatter_about(keys[8], (C,), 0.5, 3.0, jnp.float32),
    }


def group_norm_silu(values, gain, shift):
    frame_count, row_count, col_count, channels = values.shape
    per_group = channels // GROUPS
    grouped = values.reshape(frame_count, row_count, col_count, GROUPS, per_group)
    mean = lax.optimization_barrier(jnp.mean(grouped, axis=(0, 1, 2, 4)))
    centered = grouped - mean[:, None]
    var = lax.optimization_barrier(jnp.mean(centered * centered, axis=(0, 1, 2, 4)))
    inv = 1.0 / jnp.sqrt(var + 1e-06)
    normed = (centered * inv[:, None]).reshape(frame_count, row_count, col_count, channels)
    normed = normed * gain + shift
    return jax.nn.silu(normed).astype(jnp.bfloat16)

def causal_conv(acts, weight, bias):
    timed = jnp.concatenate([acts[:1], acts[:1], acts], axis=0)
    padded = jnp.pad(timed, ((0, 0), (1, 1), (1, 1), (0, 0)), mode='edge')
    result = lax.conv_general_dilated(padded[None].astype(jnp.float32), weight.astype(jnp.float32), (1, 1, 1), 'VALID', dimension_numbers=('NDHWC', 'DHWIO', 'NDHWC'), precision=lax.Precision.HIGHEST)
    return result[0] + bias

def reference(latents, gain_one, shift_one, weight_one, bias_one, gain_two, shift_two, weight_two, bias_two):
    act_one = group_norm_silu(latents.astype(jnp.float32), gain_one, shift_one)
    hidden = causal_conv(act_one, weight_one, bias_one).astype(jnp.bfloat16)
    act_two = group_norm_silu(hidden.astype(jnp.float32), gain_two, shift_two)
    branch = causal_conv(act_two, weight_two, bias_two)
    return (latents.astype(jnp.float32) + branch).astype(jnp.bfloat16)
```

```python
import functools

import jax
import jax.numpy as jnp
from jax import lax
from jax.experimental import pallas as pl
from jax.experimental.pallas import tpu as pltpu
from jax.sharding import PartitionSpec as P

GROUPS = 32
MESH = pl.DeviceIdType.MESH
F32 = jnp.float32
BF16 = jnp.bfloat16


def partial_sums(rows):
    sums, squares = [], []
    for row in rows:
        tiles = row.reshape(row.shape[0] // 8, 8, row.shape[1])
        sums.append(jnp.sum(tiles, axis=0))
        squares.append(jnp.sum(tiles * tiles, axis=0))
    total = functools.reduce(jnp.add, sums)
    square = functools.reduce(jnp.add, squares)
    return jnp.concatenate(
        [jnp.sum(total, axis=0, keepdims=True), jnp.sum(square, axis=0, keepdims=True)], axis=0
    )


def group_total(sums, per_group):
    lane = lax.broadcasted_iota(jnp.int32, sums.shape, 1)
    lanes = sums.shape[1]
    step = 1
    while step < per_group:
        up = pltpu.roll(sums, lanes - step, 1)
        down = pltpu.roll(sums, step, 1)
        sums = sums + jnp.where((lane // step) % 2 == 0, up, down)
        step *= 2
    return sums


def scale_offset(slots, gain, shift, count, per_group):
    totals = group_total(jnp.sum(slots, axis=0), per_group)
    mean = totals[0:1] / count
    var = totals[1:2] / count - mean * mean
    scale = gain / jnp.sqrt(var + 1e-06)
    return scale, shift - mean * scale


def silu(values):
    return values / (1.0 + jnp.exp(-values))


def kernel(
    n,
    count,
    per_group,
    x_hbm, g1_hbm, s1_hbm, w1_hbm, b1_hbm, g2_hbm, s2_hbm, w2_hbm, b2_hbm,
    out_ref,
    x, w1, w2, wp1, wp2, vec, act, stack, hid, own_stat, in_stat,
    load_sem, stat_send, stat_recv, rim_send, rim_recv,
):
    me = lax.axis_index("rows")
    rows = x_hbm.shape[1]
    width = x_hbm.shape[2]
    chan = x_hbm.shape[3]
    band = 3 * chan
    vec_hbm = (g1_hbm, s1_hbm, b1_hbm, g2_hbm, s2_hbm, b2_hbm)

    loads = [pltpu.make_async_copy(x_hbm.at[0], x.at[pl.ds(2, rows)], load_sem.at[0])]
    loads.append(pltpu.make_async_copy(w1_hbm, w1, load_sem.at[1]))
    loads.append(pltpu.make_async_copy(w2_hbm, w2, load_sem.at[2]))
    for i, ref in enumerate(vec_hbm):
        loads.append(pltpu.make_async_copy(ref, vec.at[i], load_sem.at[3 + i]))
    for copy in loads:
        copy.start()

    barrier = pltpu.get_barrier_semaphore()

    def greet(k, carry):
        pl.semaphore_signal(
            barrier, inc=1, device_id={"rows": lax.rem(me + k, n)}, device_id_type=MESH
        )
        return carry

    lax.fori_loop(1, n, greet, 0)

    loads[0].wait()
    own_stat[0] = partial_sums([x[2 + r].astype(F32) for r in range(rows)])

    pl.semaphore_wait(barrier, n - 1)

    def send_stats(which):
        def send(k, carry):
            pltpu.make_async_remote_copy(
                src_ref=own_stat.at[which],
                dst_ref=in_stat.at[which, k],
                send_sem=stat_send.at[which],
                recv_sem=stat_recv.at[which],
                device_id={"rows": lax.rem(me + k, n)},
                device_id_type=MESH,
            ).start()
            return carry

        lax.fori_loop(1, n, send, 0)
        in_stat[which, 0] = own_stat[which]

    def all_stats(which):
        return pltpu.make_async_remote_copy(
            src_ref=in_stat.at[which, pl.ds(1, n - 1)],
            dst_ref=in_stat.at[which, pl.ds(1, n - 1)],
            send_sem=stat_send.at[which],
            recv_sem=stat_recv.at[which],
            device_id={"rows": lax.rem(me + 1, n)},
            device_id_type=MESH,
        )

    send_stats(0)

    upward = pltpu.make_async_remote_copy(
        src_ref=x.at[pl.ds(2, 2)],
        dst_ref=x.at[pl.ds(2 + rows, 2)],
        send_sem=rim_send.at[0],
        recv_sem=rim_recv.at[0],
        device_id={"rows": lax.rem(me + n - 1, n)},
        device_id_type=MESH,
    )
    downward = pltpu.make_async_remote_copy(
        src_ref=x.at[pl.ds(rows, 2)],
        dst_ref=x.at[pl.ds(0, 2)],
        send_sem=rim_send.at[1],
        recv_sem=rim_recv.at[1],
        device_id={"rows": lax.rem(me + 1, n)},
        device_id_type=MESH,
    )

    @pl.when(me > 0)
    def _():
        upward.start()

    @pl.when(me < n - 1)
    def _():
        downward.start()

    def pair_weights(w, wp):
        zero = jnp.zeros((band, chan), BF16)
        wp[pl.ds(3 * band, band), pl.ds(0, chan)] = zero
        wp[pl.ds(0, band), pl.ds(chan, chan)] = zero
        for tap in range(3):
            at = pl.ds(tap * band, band)
            total = w[0, at].astype(F32) + w[1, at].astype(F32) + w[2, at].astype(F32)
            total = total.astype(BF16)
            wp[at, pl.ds(0, chan)] = total
            wp[pl.ds((tap + 1) * band, band), pl.ds(chan, chan)] = total

    loads[1].wait()
    pair_weights(w1, wp1)
    loads[2].wait()
    pair_weights(w2, wp2)
    for copy in loads[3:]:
        copy.wait()

    @pl.when(me == 0)
    def _():
        for r in range(2):
            x[r] = x[2]

    @pl.when(me == n - 1)
    def _():
        for r in range(2):
            x[2 + rows + r] = x[1 + rows]

    all_stats(0).wait_recv()
    scale, offset = scale_offset(in_stat[0], vec[0], vec[1], count, per_group)

    def activate(row, slot, scale, offset):
        value = silu(row.astype(F32) * scale + offset)
        act[slot, pl.ds(8, width)] = value
        act[slot, pl.ds(7, 1)] = value[0:1]
        act[slot, pl.ds(8 + width, 1)] = value[width - 1 : width]
        base = slot * band
        stack[:, pl.ds(base, chan)] = act[slot, pl.ds(7, width)].astype(BF16)
        stack[:, pl.ds(base + chan, chan)] = value.astype(BF16)
        stack[:, pl.ds(base + 2 * chan, chan)] = act[slot, pl.ds(9, width)].astype(BF16)

    for r in range(2, 2 + rows):
        activate(x[r], r, scale, offset)

    @pl.when(me < n - 1)
    def _():
        upward.wait_recv()

    @pl.when(me > 0)
    def _():
        downward.wait_recv()

    activate(x[1], 1, scale, offset)
    activate(x[2 + rows], 2 + rows, scale, offset)

    def conv_pairs(wp, first, bias):
        out = []
        for pair in range(rows // 2):
            lhs = stack[:, pl.ds((first + 2 * pair) * band, 4 * band)]
            both = jnp.dot(lhs, wp[...], preferred_element_type=F32)
            out.append(both[:, :chan] + bias)
            out.append(both[:, chan:] + bias)
        return out

    hidden = [h.astype(BF16) for h in conv_pairs(wp1, 1, vec[2])]
    for r in range(rows):
        hid[1 + r] = hidden[r]
    own_stat[1] = partial_sums([h.astype(F32) for h in hidden])
    send_stats(1)

    activate(x[0], 0, scale, offset)
    activate(x[3 + rows], 3 + rows, scale, offset)
    for target, first, edge, own in ((0, 0, 0, 1), (1 + rows, 1 + rows, n - 1, rows)):
        lhs = stack[:, pl.ds(first * band, 3 * band)]
        rim = jnp.dot(lhs, wp1[pl.ds(0, 3 * band), pl.ds(0, chan)], preferred_element_type=F32)
        rim = (rim + vec[2]).astype(BF16)
        hid[target] = rim

        @pl.when(me == edge)
        def _():
            hid[target] = hid[own]

    all_stats(1).wait_recv()
    scale, offset = scale_offset(in_stat[1], vec[3], vec[4], count, per_group)
    for r in range(rows + 2):
        activate(hid[r], r, scale, offset)
    branch = conv_pairs(wp2, 0, vec[5])
    for r in range(rows):
        out_ref[0, r] = (x[2 + r].astype(F32) + branch[r]).astype(BF16)

    all_stats(0).wait_send()
    all_stats(1).wait_send()

    @pl.when(me > 0)
    def _():
        upward.wait_send()

    @pl.when(me < n - 1)
    def _():
        downward.wait_send()


def body(latents, gain_one, shift_one, weight_one, bias_one, gain_two, shift_two, weight_two, bias_two):
    n = lax.axis_size("rows")
    frames, rows, width, chan = latents.shape
    per_group = chan // GROUPS
    count = frames * rows * width * per_group * n
    taps = weight_one.shape[0]
    flat = lambda w: w.reshape(taps, 9 * chan, chan)
    line = lambda v: v.reshape(1, chan)
    band = 3 * chan
    anywhere = pl.BlockSpec(memory_space=pltpu.HBM)
    return pl.pallas_call(
        functools.partial(kernel, n, count, per_group),
        out_shape=jax.ShapeDtypeStruct(latents.shape, BF16),
        in_specs=[anywhere] * 9,
        out_specs=pl.BlockSpec(memory_space=pltpu.VMEM),
        scratch_shapes=[
            pltpu.VMEM((rows + 4, width, chan), BF16),
            pltpu.VMEM((taps, 9 * chan, chan), BF16),
            pltpu.VMEM((taps, 9 * chan, chan), BF16),
            pltpu.VMEM((4 * band, 2 * chan), BF16),
            pltpu.VMEM((4 * band, 2 * chan), BF16),
            pltpu.VMEM((6, 1, chan), F32),
            pltpu.VMEM((rows + 4, width + 16, chan), F32),
            pltpu.VMEM((width, (rows + 4) * band), BF16),
            pltpu.VMEM((rows + 2, width, chan), BF16),
            pltpu.VMEM((2, 2, chan), F32),
            pltpu.VMEM((2, n, 2, chan), F32),
            pltpu.SemaphoreType.DMA((9,)),
            pltpu.SemaphoreType.DMA((2,)),
            pltpu.SemaphoreType.DMA((2,)),
            pltpu.SemaphoreType.DMA((2,)),
            pltpu.SemaphoreType.DMA((2,)),
        ],
        compiler_params=pltpu.CompilerParams(
            collective_id=0, has_side_effects=True, vmem_limit_bytes=48 * 1024 * 1024
        ),
    )(
        latents, line(gain_one), line(shift_one), flat(weight_one), line(bias_one),
        line(gain_two), line(shift_two), flat(weight_two), line(bias_two),
    )


def solution(mesh):
    return jax.shard_map(
        body,
        mesh=mesh,
        in_specs=(P("groups", "rows", None, None), P(), P(), P(), P(), P(), P(), P(), P()),
        out_specs=P("groups", "rows", None, None),
        check_vma=False,
    )
```

```python
import functools

import jax
import jax.numpy as jnp
from jax import lax
from jax.experimental import pallas as pl
from jax.experimental.pallas import tpu as pltpu
from jax.sharding import PartitionSpec as P

GROUPS = 32
MESH = pl.DeviceIdType.MESH
F32 = jnp.float32
BF16 = jnp.bfloat16
VMEM_BYTES = (64 * 1024 - 10720) * 1024


def partial_sums(rows):
    sums, squares = [], []
    for row in rows:
        tiles = row.reshape(row.shape[0] // 8, 8, row.shape[1])
        sums.append(jnp.sum(tiles, axis=0))
        squares.append(jnp.sum(tiles * tiles, axis=0))
    total = functools.reduce(jnp.add, sums)
    square = functools.reduce(jnp.add, squares)
    return jnp.concatenate(
        [jnp.sum(total, axis=0, keepdims=True), jnp.sum(square, axis=0, keepdims=True)], axis=0
    )


def group_total(sums, per_group):
    lane = lax.broadcasted_iota(jnp.int32, sums.shape, 1)
    lanes = sums.shape[1]
    step = 1
    while step < per_group:
        up = pltpu.roll(sums, lanes - step, 1)
        down = pltpu.roll(sums, step, 1)
        sums = sums + jnp.where((lane // step) % 2 == 0, up, down)
        step *= 2
    return sums


def scale_offset(slots, gain, shift, count, per_group):
    totals = group_total(jnp.sum(slots, axis=0), per_group)
    mean = totals[0:1] / count
    var = totals[1:2] / count - mean * mean
    scale = (0.5 * gain) / jnp.sqrt(var + 1e-06)
    return scale, 0.5 * shift - mean * scale


def silu_of_double(half):
    return half + half * jnp.tanh(half)


def kernel(
    n,
    count,
    per_group,
    x_hbm, g1_hbm, s1_hbm, w1_hbm, b1_hbm, g2_hbm, s2_hbm, w2_hbm, b2_hbm,
    out_ref,
    x, w1, w2, wp1, wp2, vec, act, stack, hid, own_stat, in_stat,
    load_sem, stat_send, stat_recv, rim_send, rim_recv,
):
    me = lax.axis_index("rows")
    rows = x_hbm.shape[1]
    width = x_hbm.shape[2]
    chan = x_hbm.shape[3]
    band = 3 * chan
    vec_hbm = (g1_hbm, s1_hbm, b1_hbm, g2_hbm, s2_hbm, b2_hbm)

    low = jnp.where(me < n // 2, 1, 0)

    def other(k):
        place = low * (n - 1 - k) + (1 - low) * k
        return place + jnp.where(low == 1, jnp.where(place <= me, -1, 0), jnp.where(place >= me, 1, 0))

    barrier = pltpu.get_barrier_semaphore()

    def greet(k, carry):
        pl.semaphore_signal(barrier, inc=1, device_id={"rows": other(k)}, device_id_type=MESH)
        return carry

    lax.fori_loop(0, n - 1, greet, 0)

    loads = [pltpu.make_async_copy(x_hbm.at[0], x.at[pl.ds(2, rows)], load_sem.at[0])]
    loads.append(pltpu.make_async_copy(w1_hbm, w1, load_sem.at[1]))
    loads.append(pltpu.make_async_copy(w2_hbm, w2, load_sem.at[2]))
    for i, ref in enumerate(vec_hbm):
        loads.append(pltpu.make_async_copy(ref, vec.at[i], load_sem.at[3 + i]))
    for copy in loads:
        copy.start()

    pl.semaphore_wait(barrier, n - 1)

    up_id = {"rows": lax.rem(me + n - 1, n)}
    down_id = {"rows": lax.rem(me + 1, n)}

    def rim(source, target, device, sem):
        return pltpu.make_async_remote_copy(
            src_ref=x_hbm.at[0, pl.ds(source, 1)],
            dst_ref=x.at[pl.ds(target, 1)],
            send_sem=rim_send.at[sem],
            recv_sem=rim_recv.at[sem],
            device_id=device,
            device_id_type=MESH,
        )

    upward = [rim(i, 2 + rows + i, up_id, i) for i in range(2)]
    downward = [rim(rows - 1 - i, 1 - i, down_id, 2 + i) for i in range(2)]
    for i in range(2):

        @pl.when(me > 0)
        def _():
            upward[i].start()

        @pl.when(me < n - 1)
        def _():
            downward[i].start()

    def rims_arrive(i):
        @pl.when(me < n - 1)
        def _():
            upward[i].wait_recv()

        @pl.when(me > 0)
        def _():
            downward[i].wait_recv()

    def send_stats(which):
        def send(k, carry):
            target = other(k)
            pltpu.make_async_remote_copy(
                src_ref=own_stat.at[which],
                dst_ref=in_stat.at[which, me],
                send_sem=stat_send.at[which],
                recv_sem=stat_recv.at[which],
                device_id={"rows": target},
                device_id_type=MESH,
            ).start()
            return carry

        lax.fori_loop(0, n - 1, send, 0)
        in_stat[which, me] = own_stat[which]

    def all_stats(which):
        return pltpu.make_async_remote_copy(
            src_ref=in_stat.at[which, pl.ds(1, n - 1)],
            dst_ref=in_stat.at[which, pl.ds(1, n - 1)],
            send_sem=stat_send.at[which],
            recv_sem=stat_recv.at[which],
            device_id={"rows": lax.rem(me + 1, n)},
            device_id_type=MESH,
        )

    loads[0].wait()
    own_stat[0] = partial_sums([x[2 + r].astype(F32) for r in range(rows)])
    send_stats(0)

    def pair_weights(w, wp):
        zero = jnp.zeros((band, chan), BF16)
        wp[pl.ds(3 * band, band), pl.ds(0, chan)] = zero
        wp[pl.ds(0, band), pl.ds(chan, chan)] = zero
        for tap in range(3):
            at = pl.ds(tap * band, band)
            total = w[0, at].astype(F32) + w[1, at].astype(F32) + w[2, at].astype(F32)
            total = total.astype(BF16)
            wp[at, pl.ds(0, chan)] = total
            wp[pl.ds((tap + 1) * band, band), pl.ds(chan, chan)] = total

    loads[1].wait()
    pair_weights(w1, wp1)
    loads[2].wait()
    pair_weights(w2, wp2)
    for copy in loads[3:]:
        copy.wait()

    @pl.when(me == 0)
    def _():
        for r in range(2):
            x[r] = x[2]

    @pl.when(me == n - 1)
    def _():
        for r in range(2):
            x[2 + rows + r] = x[1 + rows]

    all_stats(0).wait_recv()
    scale, offset = scale_offset(in_stat[0], vec[0], vec[1], count, per_group)

    def activate(row, slot, scale, offset):
        value = silu_of_double(row.astype(F32) * scale + offset)
        act[slot, pl.ds(8, width)] = value
        act[slot, pl.ds(7, 1)] = value[0:1]
        act[slot, pl.ds(8 + width, 1)] = value[width - 1 : width]
        base = slot * band
        stack[:, pl.ds(base, chan)] = act[slot, pl.ds(7, width)].astype(BF16)
        stack[:, pl.ds(base + chan, chan)] = value.astype(BF16)
        stack[:, pl.ds(base + 2 * chan, chan)] = act[slot, pl.ds(9, width)].astype(BF16)

    for r in range(2, 2 + rows):
        activate(x[r], r, scale, offset)

    rims_arrive(0)
    activate(x[1], 1, scale, offset)
    activate(x[2 + rows], 2 + rows, scale, offset)

    def conv_pairs(wp, first, bias):
        out = []
        for pair in range(rows // 2):
            lhs = stack[:, pl.ds((first + 2 * pair) * band, 4 * band)]
            both = jnp.dot(lhs, wp[...], preferred_element_type=F32)
            out.append(both[:, :chan] + bias)
            out.append(both[:, chan:] + bias)
        return out

    hidden = [h.astype(BF16) for h in conv_pairs(wp1, 1, vec[2])]
    for r in range(rows):
        hid[1 + r] = hidden[r]
    own_stat[1] = partial_sums([h.astype(F32) for h in hidden])
    send_stats(1)

    rims_arrive(1)
    activate(x[0], 0, scale, offset)
    activate(x[3 + rows], 3 + rows, scale, offset)
    for target, first, edge, own in ((0, 0, 0, 1), (1 + rows, 1 + rows, n - 1, rows)):
        lhs = stack[:, pl.ds(first * band, 3 * band)]
        rim = jnp.dot(lhs, wp1[pl.ds(0, 3 * band), pl.ds(0, chan)], preferred_element_type=F32)
        rim = (rim + vec[2]).astype(BF16)
        hid[target] = rim

        @pl.when(me == edge)
        def _():
            hid[target] = hid[own]

    all_stats(1).wait_recv()
    scale, offset = scale_offset(in_stat[1], vec[3], vec[4], count, per_group)
    for r in range(rows + 2):
        activate(hid[r], r, scale, offset)
    branch = conv_pairs(wp2, 0, vec[5])
    for r in range(rows):
        out_ref[0, r] = (x[2 + r].astype(F32) + branch[r]).astype(BF16)

    all_stats(0).wait_send()
    all_stats(1).wait_send()

    for i in range(2):

        @pl.when(me > 0)
        def _():
            upward[i].wait_send()

        @pl.when(me < n - 1)
        def _():
            downward[i].wait_send()


def body(latents, gain_one, shift_one, weight_one, bias_one, gain_two, shift_two, weight_two, bias_two):
    n = lax.axis_size("rows")
    frames, rows, width, chan = latents.shape
    per_group = chan // GROUPS
    count = frames * rows * width * per_group * n
    taps = weight_one.shape[0]
    flat = lambda w: w.reshape(taps, 9 * chan, chan)
    line = lambda v: v.reshape(1, chan)
    band = 3 * chan
    anywhere = pl.BlockSpec(memory_space=pl.ANY)
    return pl.pallas_call(
        functools.partial(kernel, n, count, per_group),
        out_shape=jax.ShapeDtypeStruct(latents.shape, BF16),
        in_specs=[anywhere] * 9,
        out_specs=pl.BlockSpec(memory_space=pltpu.VMEM),
        scratch_shapes=[
            pltpu.VMEM((rows + 4, width, chan), BF16),
            pltpu.VMEM((taps, 9 * chan, chan), BF16),
            pltpu.VMEM((taps, 9 * chan, chan), BF16),
            pltpu.VMEM((4 * band, 2 * chan), BF16),
            pltpu.VMEM((4 * band, 2 * chan), BF16),
            pltpu.VMEM((6, 1, chan), F32),
            pltpu.VMEM((rows + 4, width + 16, chan), F32),
            pltpu.VMEM((width, (rows + 4) * band), BF16),
            pltpu.VMEM((rows + 2, width, chan), BF16),
            pltpu.VMEM((2, 2, chan), F32),
            pltpu.VMEM((2, n, 2, chan), F32),
            pltpu.SemaphoreType.DMA((9,)),
            pltpu.SemaphoreType.DMA((2,)),
            pltpu.SemaphoreType.DMA((2,)),
            pltpu.SemaphoreType.DMA((4,)),
            pltpu.SemaphoreType.DMA((4,)),
        ],
        compiler_params=pltpu.CompilerParams(
            collective_id=0, has_side_effects=True, vmem_limit_bytes=VMEM_BYTES
        ),
    )(
        latents, line(gain_one), line(shift_one), flat(weight_one), line(bias_one),
        line(gain_two), line(shift_two), flat(weight_two), line(bias_two),
    )


def solution(mesh):
    return jax.shard_map(
        body,
        mesh=mesh,
        in_specs=(P("groups", "rows", None, None), P(), P(), P(), P(), P(), P(), P(), P()),
        out_specs=P("groups", "rows", None, None),
        check_vma=False,
    )
```

```python
import functools

import jax
import jax.numpy as jnp
from jax import lax
from jax.experimental import pallas as pl
from jax.experimental.pallas import tpu as pltpu
from jax.sharding import PartitionSpec as P

GROUPS = 32
MESH = pl.DeviceIdType.MESH
F32 = jnp.float32
BF16 = jnp.bfloat16
VMEM_BYTES = (64 * 1024 - 10720) * 1024


def partial_sums(rows):
    sums, squares = [], []
    for row in rows:
        tiles = row.reshape(row.shape[0] // 8, 8, row.shape[1])
        sums.append(jnp.sum(tiles, axis=0))
        squares.append(jnp.sum(tiles * tiles, axis=0))
    total = functools.reduce(jnp.add, sums)
    square = functools.reduce(jnp.add, squares)
    return jnp.concatenate(
        [jnp.sum(total, axis=0, keepdims=True), jnp.sum(square, axis=0, keepdims=True)], axis=0
    )


def group_total(sums, per_group):
    lane = lax.broadcasted_iota(jnp.int32, sums.shape, 1)
    lanes = sums.shape[1]
    step = 1
    while step < per_group:
        up = pltpu.roll(sums, lanes - step, 1)
        down = pltpu.roll(sums, step, 1)
        sums = sums + jnp.where((lane // step) % 2 == 0, up, down)
        step *= 2
    return sums


def scale_offset(slots, gain, shift, count, per_group):
    totals = group_total(jnp.sum(slots, axis=0), per_group)
    mean = totals[0:1] / count
    var = totals[1:2] / count - mean * mean
    scale = (0.5 * gain) / jnp.sqrt(var + 1e-06)
    return scale, 0.5 * shift - mean * scale


def silu_of_double(half):
    return half + half * jnp.tanh(half)


def kernel(
    n,
    count,
    per_group,
    x_hbm, g1_hbm, s1_hbm, w1_hbm, b1_hbm, g2_hbm, s2_hbm, w2_hbm, b2_hbm,
    out_ref,
    x, w1, w2, wp1, wp2, vec, act, stack, hid, own_stat, in_stat,
    load_sem, stat_send, stat_recv, rim_send, rim_recv,
):
    me = lax.axis_index("rows")
    rows = x_hbm.shape[1]
    width = x_hbm.shape[2]
    chan = x_hbm.shape[3]
    band = 3 * chan
    vec_hbm = (g1_hbm, s1_hbm, b1_hbm, g2_hbm, s2_hbm, b2_hbm)

    low = jnp.where(me < n // 2, 1, 0)

    def other(k):
        place = low * (n - 1 - k) + (1 - low) * k
        return place + jnp.where(low == 1, jnp.where(place <= me, -1, 0), jnp.where(place >= me, 1, 0))

    barrier = pltpu.get_barrier_semaphore()

    def greet(k, carry):
        pl.semaphore_signal(barrier, inc=1, device_id={"rows": other(k)}, device_id_type=MESH)
        return carry

    lax.fori_loop(0, n - 1, greet, 0)

    loads = [pltpu.make_async_copy(x_hbm.at[0], x.at[pl.ds(2, rows)], load_sem.at[0])]
    loads.append(pltpu.make_async_copy(w1_hbm, w1, load_sem.at[1]))
    loads.append(pltpu.make_async_copy(w2_hbm, w2, load_sem.at[2]))
    for i, ref in enumerate(vec_hbm):
        loads.append(pltpu.make_async_copy(ref, vec.at[i], load_sem.at[3 + i]))
    for copy in loads:
        copy.start()

    pl.semaphore_wait(barrier, n - 1)

    up_id = {"rows": lax.rem(me + n - 1, n)}
    down_id = {"rows": lax.rem(me + 1, n)}

    def rim(source, target, device, sem):
        return pltpu.make_async_remote_copy(
            src_ref=x_hbm.at[0, pl.ds(source, 1)],
            dst_ref=x.at[pl.ds(target, 1)],
            send_sem=rim_send.at[sem],
            recv_sem=rim_recv.at[sem],
            device_id=device,
            device_id_type=MESH,
        )

    upward = [rim(i, 2 + rows + i, up_id, i) for i in range(2)]
    downward = [rim(rows - 1 - i, 1 - i, down_id, 2 + i) for i in range(2)]
    def send_rims(i):
        @pl.when(me > 0)
        def _():
            upward[i].start()

        @pl.when(me < n - 1)
        def _():
            downward[i].start()

    def rims_arrive(i):
        @pl.when(me < n - 1)
        def _():
            upward[i].wait_recv()

        @pl.when(me > 0)
        def _():
            downward[i].wait_recv()

    def send_stats(which):
        def send(k, carry):
            target = other(k)
            pltpu.make_async_remote_copy(
                src_ref=own_stat.at[which],
                dst_ref=in_stat.at[which, me],
                send_sem=stat_send.at[which],
                recv_sem=stat_recv.at[which],
                device_id={"rows": target},
                device_id_type=MESH,
            ).start()
            return carry

        lax.fori_loop(0, n - 1, send, 0)
        in_stat[which, me] = own_stat[which]

    def all_stats(which):
        return pltpu.make_async_remote_copy(
            src_ref=in_stat.at[which, pl.ds(1, n - 1)],
            dst_ref=in_stat.at[which, pl.ds(1, n - 1)],
            send_sem=stat_send.at[which],
            recv_sem=stat_recv.at[which],
            device_id={"rows": lax.rem(me + 1, n)},
            device_id_type=MESH,
        )

    loads[0].wait()
    own_stat[0] = partial_sums([x[2 + r].astype(F32) for r in range(rows)])
    send_stats(0)
    send_rims(0)
    send_rims(1)

    def pair_weights(w, wp):
        zero = jnp.zeros((band, chan), BF16)
        wp[pl.ds(3 * band, band), pl.ds(0, chan)] = zero
        wp[pl.ds(0, band), pl.ds(chan, chan)] = zero
        for tap in range(3):
            at = pl.ds(tap * band, band)
            total = w[0, at].astype(F32) + w[1, at].astype(F32) + w[2, at].astype(F32)
            total = total.astype(BF16)
            wp[at, pl.ds(0, chan)] = total
            wp[pl.ds((tap + 1) * band, band), pl.ds(chan, chan)] = total

    loads[1].wait()
    pair_weights(w1, wp1)
    for copy in loads[3:]:
        copy.wait()

    @pl.when(me == 0)
    def _():
        for r in range(2):
            x[r] = x[2]

    @pl.when(me == n - 1)
    def _():
        for r in range(2):
            x[2 + rows + r] = x[1 + rows]

    all_stats(0).wait_recv()
    scale, offset = scale_offset(in_stat[0], vec[0], vec[1], count, per_group)

    def activate(row, slot, scale, offset):
        value = silu_of_double(row.astype(F32) * scale + offset)
        act[slot, pl.ds(8, width)] = value
        act[slot, pl.ds(7, 1)] = value[0:1]
        act[slot, pl.ds(8 + width, 1)] = value[width - 1 : width]
        base = slot * band
        stack[:, pl.ds(base, chan)] = act[slot, pl.ds(7, width)].astype(BF16)
        stack[:, pl.ds(base + chan, chan)] = value.astype(BF16)
        stack[:, pl.ds(base + 2 * chan, chan)] = act[slot, pl.ds(9, width)].astype(BF16)

    for r in range(2, 2 + rows):
        activate(x[r], r, scale, offset)

    rims_arrive(0)
    activate(x[1], 1, scale, offset)
    activate(x[2 + rows], 2 + rows, scale, offset)

    def conv_pairs(wp, first, bias):
        out = []
        for pair in range(rows // 2):
            lhs = stack[:, pl.ds((first + 2 * pair) * band, 4 * band)]
            both = jnp.dot(lhs, wp[...], preferred_element_type=F32)
            out.append(both[:, :chan] + bias)
            out.append(both[:, chan:] + bias)
        return out

    hidden = [h.astype(BF16) for h in conv_pairs(wp1, 1, vec[2])]
    for r in range(rows):
        hid[1 + r] = hidden[r]
    own_stat[1] = partial_sums([h.astype(F32) for h in hidden])
    send_stats(1)

    loads[2].wait()
    pair_weights(w2, wp2)
    rims_arrive(1)
    activate(x[0], 0, scale, offset)
    activate(x[3 + rows], 3 + rows, scale, offset)
    for target, first, edge, own in ((0, 0, 0, 1), (1 + rows, 1 + rows, n - 1, rows)):
        lhs = stack[:, pl.ds(first * band, 3 * band)]
        rim = jnp.dot(lhs, wp1[pl.ds(0, 3 * band), pl.ds(0, chan)], preferred_element_type=F32)
        rim = (rim + vec[2]).astype(BF16)
        hid[target] = rim

        @pl.when(me == edge)
        def _():
            hid[target] = hid[own]

    all_stats(1).wait_recv()
    scale, offset = scale_offset(in_stat[1], vec[3], vec[4], count, per_group)
    for r in range(rows + 2):
        activate(hid[r], r, scale, offset)
    branch = conv_pairs(wp2, 0, vec[5])
    for r in range(rows):
        out_ref[0, r] = (x[2 + r].astype(F32) + branch[r]).astype(BF16)

    all_stats(0).wait_send()
    all_stats(1).wait_send()

    for i in range(2):

        @pl.when(me > 0)
        def _():
            upward[i].wait_send()

        @pl.when(me < n - 1)
        def _():
            downward[i].wait_send()


def body(latents, gain_one, shift_one, weight_one, bias_one, gain_two, shift_two, weight_two, bias_two):
    n = lax.axis_size("rows")
    frames, rows, width, chan = latents.shape
    per_group = chan // GROUPS
    count = frames * rows * width * per_group * n
    taps = weight_one.shape[0]
    flat = lambda w: w.reshape(taps, 9 * chan, chan)
    line = lambda v: v.reshape(1, chan)
    band = 3 * chan
    anywhere = pl.BlockSpec(memory_space=pl.ANY)
    return pl.pallas_call(
        functools.partial(kernel, n, count, per_group),
        out_shape=jax.ShapeDtypeStruct(latents.shape, BF16),
        in_specs=[anywhere] * 9,
        out_specs=pl.BlockSpec(memory_space=pltpu.VMEM),
        scratch_shapes=[
            pltpu.VMEM((rows + 4, width, chan), BF16),
            pltpu.VMEM((taps, 9 * chan, chan), BF16),
            pltpu.VMEM((taps, 9 * chan, chan), BF16),
            pltpu.VMEM((4 * band, 2 * chan), BF16),
            pltpu.VMEM((4 * band, 2 * chan), BF16),
            pltpu.VMEM((6, 1, chan), F32),
            pltpu.VMEM((rows + 4, width + 16, chan), F32),
            pltpu.VMEM((width, (rows + 4) * band), BF16),
            pltpu.VMEM((rows + 2, width, chan), BF16),
            pltpu.VMEM((2, 2, chan), F32),
            pltpu.VMEM((2, n, 2, chan), F32),
            pltpu.SemaphoreType.DMA((9,)),
            pltpu.SemaphoreType.DMA((2,)),
            pltpu.SemaphoreType.DMA((2,)),
            pltpu.SemaphoreType.DMA((4,)),
            pltpu.SemaphoreType.DMA((4,)),
        ],
        compiler_params=pltpu.CompilerParams(
            collective_id=0, has_side_effects=True, vmem_limit_bytes=VMEM_BYTES
        ),
    )(
        latents, line(gain_one), line(shift_one), flat(weight_one), line(bias_one),
        line(gain_two), line(shift_two), flat(weight_two), line(bias_two),
    )


def solution(mesh):
    return jax.shard_map(
        body,
        mesh=mesh,
        in_specs=(P("groups", "rows", None, None), P(), P(), P(), P(), P(), P(), P(), P()),
        out_specs=P("groups", "rows", None, None),
        check_vma=False,
    )
```
